256 devices in a mesh: lon: 256 (over x, y, z, core).
Axes of the slice: x: 4, y: 4, z: 8, core: 2. Of those that a mesh axis runs over, the one named last changes fastest.
Arguments:
- field: float32 [16, 13312, 200], P(None, 'lon'), may hold values from -6 to 6
- south_rows: float32 [8, 13312, 200], P(None, 'lon'), may hold values from -6 to 6
- sign_mask: int32 [200], replicated, may hold values from -1 to 1, as said below
- weights: float32 [4, 9, 200, 200], replicated, may hold values from -0.125 to 0.125
- biases: float32 [4, 200], replicated, may hold values from -3 to 3
Outputs:
- result: float32 [16, 13312, 200], P(None, 'lon')
The draws below stay inside these ranges and needn't reach their ends.
Inputs may be any that keep to these rules, and one draw needn't show every extreme that they name: `sign_mask`: every entry is +1 or -1.
All inputs are finite; a program needn't handle non-finite values.
Results may differ from the reference program's by a relative error of at most 0.0001.
Values sent between devices are 32-bit elements; how exact they have to be, the bound alone decides.
A program may use at most 64 MiB of HBM per device.

```python
import jax
import jax.numpy as jnp
from jax import lax

C = 200
R = 16
LAYERS = 4
NLON = 13312
SOUTH = 8


def draw_sign_mask(key, part):
    return (2 * jax.random.randint(key, (C,), 0, 2) - 1).astype(jnp.int32)


def block_levels(stream_key, extent, cuts, smallest, top_value):
    def one(dim, blocks):
        draws = jax.random.uniform(jax.random.fold_in(jax.random.fold_in(stream_key, 6), dim), (blocks,), jnp.float32, smallest / len(cuts), top_value / len(cuts))
        return jnp.repeat(jnp.exp(draws), extent[dim] // blocks).reshape((-1,) + (1,) * (len(extent) - dim - 1))

    loudness = one(*cuts[0])
    for cut in cuts[1:]:
        loudness = loudness * one(*cut)
    return loudness


def centred(stream_key, shape, deviation, reach, pieces=(), kind=jnp.bfloat16):
    factor_of = block_levels(stream_key, shape, pieces, -0.22, 0.18) if pieces else 1.0
    result = jax.random.normal(stream_key, shape, jnp.float32) * deviation * factor_of
    return jnp.minimum(jnp.maximum(result, -reach), reach).astype(kind)


def setup_inputs(seed: int = 0) -> dict:
    arg_keys = jax.random.split(jax.random.key(seed), 6)
    return {
        "field": centred(arg_keys[0], (R, NLON, C), 1.0, 6.0, ((1, 256),), jnp.float32),
        "south_rows": centred(arg_keys[1], (SOUTH, NLON, C), 1.0, 6.0, ((1, 256),), jnp.float32),
        "sign_mask": draw_sign_mask(jax.random.fold_in(arg_keys[5], 71), 0),
        "weights": centred(arg_keys[3], (LAYERS, 9, C, C), (9 * C) ** -0.5, 0.125, (), jnp.float32),
        "biases": centred(arg_keys[4], (LAYERS, C), 0.5, 3.0, (), jnp.float32),
    }


def convolve(padded, kernel, offset, dilate, row_count, col_count):
    summed = jnp.zeros((row_count, col_count, kernel.shape[-1]), jnp.float32)
    for tap_row in range(3):
        for tap_col in range(3):
            window = padded[tap_row * dilate:tap_row * dilate + row_count, tap_col * dilate:tap_col * dilate + col_count]
            summed = summed + jnp.einsum("rlc,cd->rld", window, kernel[3 * tap_row + tap_col], precision=lax.Precision.HIGHEST)
    return summed + offset


def reference(field, south_rows, sign_mask, weights, biases):
    row_count, col_count = field.shape[0], field.shape[1]
    channel_signs = sign_mask.astype(jnp.float32)
    for layer_index in range(weights.shape[0]):
        dilate = 2 ** layer_index
        south_part = south_rows[south_rows.shape[0] - dilate:]
        north_rows = (field[row_count - dilate:][::-1] * channel_signs)[:, ::-1]
        stacked = jnp.concatenate([south_part, field, north_rows], 0)
        padded = jnp.concatenate([stacked[:, col_count - dilate:], stacked, stacked[:, :dilate]], 1)
        field = field + jax.nn.gelu(convolve(padded, weights[layer_index], biases[layer_index], dilate, row_count, col_count))
    return field
```

```python
import functools

import jax
import jax.numpy as jnp
from jax import lax
from jax.experimental import pallas as pl
from jax.experimental.pallas import tpu as pltpu
from jax.sharding import PartitionSpec as P

MESH = pl.DeviceIdType.MESH
F32 = jnp.float32
BF16 = jnp.bfloat16
R = 16
W = 15


def reverse_rows(v):
    row = lax.broadcasted_iota(jnp.int32, v.shape, 1)
    v = pltpu.roll(v, 4, 1)
    v = jnp.where((row & 2) == 0, pltpu.roll(v, 6, 1), pltpu.roll(v, 2, 1))
    return jnp.where((row & 1) == 0, pltpu.roll(v, 7, 1), pltpu.roll(v, 1, 1))


def gelu(x):
    return 0.5 * x * (1.0 + jnp.tanh(0.7978845608028654 * (x + 0.044715 * (x * x * x))))


def kernel(ndev, n, field, south, sign, weights, bias, out, wf, wh, wl, slab, xh, xl, acc,
           wsem, lsem, ssem, rsem):
    me = lax.axis_index("lon")
    right, left, twin = lax.rem(me + 1, ndev), lax.rem(me + ndev - 1, ndev), ndev - 1 - me
    total = n + 2 * W

    loads = [pltpu.make_async_copy(weights.at[pl.ds(9 * l, 9)], wf.at[pl.ds(9 * l, 9)], wsem.at[l]) for l in range(4)]
    loads[0].start()
    own = [pltpu.make_async_copy(field, slab.at[0, 0, pl.ds(W, n), pl.ds(8, R)], lsem.at[0]),
           pltpu.make_async_copy(south, slab.at[0, 0, pl.ds(W, n), pl.ds(0, 8)], lsem.at[1])]
    for c in own:
        c.start()
    for c in loads[1:]:
        c.start()

    barrier = pltpu.get_barrier_semaphore()
    for peer in (left, right, twin):
        pl.semaphore_signal(barrier, inc=1, device_id=(peer,), device_id_type=MESH)
    pl.semaphore_wait(barrier, 3)

    def remote(src, dst, k, peer):
        return pltpu.make_async_remote_copy(src_ref=src, dst_ref=dst, send_sem=ssem.at[k], recv_sem=rsem.at[k],
                                            device_id=(peer,), device_id_type=MESH)

    fold = [remote(field.at[:, pl.ds(8, 8)], slab.at[1, 0, pl.ds(W, n), pl.ds(16, 8)], 0, twin),
            remote(field.at[:, pl.ds(0, 8)], slab.at[1, 0, pl.ds(W, n), pl.ds(8, 8)], 1, twin)]
    edge = [remote(field.at[pl.ds(n - W, W)], slab.at[0, 0, pl.ds(0, W), pl.ds(8, R)], 2, right),
            remote(field.at[pl.ds(0, W)], slab.at[0, 0, pl.ds(W + n, W), pl.ds(8, R)], 3, left),
            remote(south.at[pl.ds(n - W, W)], slab.at[0, 0, pl.ds(0, W), pl.ds(0, 8)], 4, right),
            remote(south.at[pl.ds(0, W)], slab.at[0, 0, pl.ds(W + n, W), pl.ds(0, 8)], 5, left)]

    def onward(row, k):
        rows = pl.ds(row, 8)
        return [remote(slab.at[1, 0, pl.ds(n, W), rows], slab.at[1, 0, pl.ds(0, W), rows], k, left),
                remote(slab.at[1, 0, pl.ds(W, W), rows], slab.at[1, 0, pl.ds(W + n, W), rows], k + 1, right)]

    upper, lower = onward(16, 6), onward(8, 8)

    fold[0].start()
    for c in edge:
        c.start()
    fold[1].start()

    def prepare(l):
        loads[l].wait()

        def one(t, _):
            w = wf[t]
            hi = w.astype(BF16)
            wh[t] = hi
            wl[t] = (w - hi.astype(F32)).astype(BF16)
            return 0

        lax.fori_loop(9 * l, 9 * l + 9, one, 0)

    def north(side, l):
        def one(j, _):
            v = slab[1 - side, l, pl.ds(total - 2 - 2 * j, 2), pl.ds(16, 8), :]
            v = reverse_rows(v) * sign[...]
            slab[side, l, pl.ds(2 * j, 1), pl.ds(24, 8), :] = v[1:2]
            slab[side, l, pl.ds(2 * j + 1, 1), pl.ds(24, 8), :] = v[0:1]
            return 0

        lax.fori_loop(0, total // 2, one, 0)

    def layer(l, first, second, cols):
        s = 2 ** l
        for a in range(3):
            def part(window):
                side, row, col = window
                return slab[side, l, pl.ds(col - s, cols + 2 * s), pl.ds(row + (a - 1) * s, 8), :]

            x = jnp.concatenate([part(first), part(second)], axis=1)
            hi = x.astype(BF16)
            xh[a, pl.ds(0, cols + 2 * s)] = hi
            xl[a, pl.ds(0, cols + 2 * s)] = (x - hi.astype(F32)).astype(BF16)
        size = cols * R

        def tap(i, _):
            a, b = i // 3, i % 3
            rows = pl.ds(b * s, cols)
            h = xh[a, rows].reshape(size, -1)
            lo = xl[a, rows].reshape(size, -1)
            t = 9 * l + i
            d = jnp.dot(h, wh[t], preferred_element_type=F32)
            d += jnp.dot(lo, wh[t], preferred_element_type=F32)
            d += jnp.dot(h, wl[t], preferred_element_type=F32)
            acc[pl.ds(0, size)] += d
            return 0

        acc[pl.ds(0, size)] = jnp.broadcast_to(bias[pl.ds(l, 1)], (size, acc.shape[-1]))
        lax.fori_loop(0, 9, tap, 0)
        g = gelu(acc[pl.ds(0, size)]).reshape(cols, R, -1)
        for window, lo_row in ((first, 0), (second, 8)):
            side, row, col = window
            new = slab[side, l, pl.ds(col, cols), pl.ds(row, 8), :] + g[:, lo_row:lo_row + 8]
            if l == 3:
                out[pl.ds(col - W, cols), pl.ds(row - 8, 8), :] = new
            else:
                slab[side, l + 1, pl.ds(col, cols), pl.ds(row, 8), :] = new

    zero = jnp.zeros((total, 8, slab.shape[-1]), F32)
    slab[1, 0, :, pl.ds(0, 8), :] = zero
    for l in range(4):
        prepare(l)
    for c in own:
        c.wait()
    for c in edge:
        c.wait()
    for l in range(1, 4):
        slab[0, l, :, pl.ds(0, 8), :] = slab[0, 0, :, pl.ds(0, 8), :]
        slab[1, l, :, pl.ds(0, 8), :] = zero

    low, high = (0, 8), (0, 16)
    fold[0].wait()
    for c in upper:
        c.start()
    for c in upper:
        c.wait()
    fold[1].wait()
    for c in lower:
        c.start()
    for c in lower:
        c.wait()
    c1, c2, c3 = 1, 3, 7
    n1, n2, n3 = total - 2, total - 6, total - 14
    north(0, 0)
    north(1, 0)
    layer(0, (0, 8, c1), (0, 16, c1), n1)
    layer(0, (1, 8, c1), (1, 16, c1), n1)
    north(0, 1)
    north(1, 1)
    layer(1, (0, 8, c2), (0, 16, c2), n2)
    layer(1, (1, 8, c2), (1, 16, c2), n2)
    north(0, 2)
    north(1, 2)
    layer(2, (0, 8, c3), (0, 16, c3), n3)
    layer(2, (1, 16, c3), (1, 16, c3 + n3 // 2), n3 // 2)
    north(0, 3)
    layer(3, (0, 8, W), (0, 16, W), n)


def local(ndev, field, south, sign, weights, bias):
    rows, n, c = field.shape
    total = n + 2 * W
    weights = weights.reshape(-1, c, c)
    taps = weights.shape[0]
    any_ = pl.BlockSpec(memory_space=pl.ANY)
    vmem = pl.BlockSpec(memory_space=pltpu.VMEM)
    result = pl.pallas_call(
        functools.partial(kernel, ndev, n),
        out_shape=jax.ShapeDtypeStruct((n, rows, c), F32),
        in_specs=[any_, any_, vmem, any_, vmem],
        out_specs=vmem,
        scratch_shapes=[
            pltpu.VMEM((taps, c, c), F32),
            pltpu.VMEM((taps, c, c), BF16),
            pltpu.VMEM((taps, c, c), BF16),
            pltpu.VMEM((2, 4, total, 32, c), F32),
            pltpu.VMEM((3, total, R, c), BF16),
            pltpu.VMEM((3, total, R, c), BF16),
            pltpu.VMEM(((total - 2) * R, c), F32),
            pltpu.SemaphoreType.DMA((4,)),
            pltpu.SemaphoreType.DMA((2,)),
            pltpu.SemaphoreType.DMA((10,)),
            pltpu.SemaphoreType.DMA((10,)),
        ],
        compiler_params=pltpu.CompilerParams(collective_id=0, has_side_effects=True, vmem_limit_bytes=60 << 20),
    )(field.transpose(1, 0, 2), south.transpose(1, 0, 2), sign.astype(F32).reshape(1, -1), weights, bias)
    return result.transpose(1, 0, 2)


def solution(mesh):
    ndev = mesh.shape["lon"]
    lon = P(None, "lon", None)
    return jax.shard_map(functools.partial(local, ndev), mesh=mesh, in_specs=(lon, lon, P(), P(), P()),
                         out_specs=lon, check_vma=False)
```

```python
import functools

import jax
import jax.numpy as jnp
from jax import lax
from jax.experimental import pallas as pl
from jax.experimental.pallas import tpu as pltpu
from jax.sharding import PartitionSpec as P

MESH = pl.DeviceIdType.MESH
F32 = jnp.float32
BF16 = jnp.bfloat16
R = 16
PIECE = 20
W = 15


def reverse_rows(v):
    row = lax.broadcasted_iota(jnp.int32, v.shape, 1)
    v = pltpu.roll(v, 4, 1)
    v = jnp.where((row & 2) == 0, pltpu.roll(v, 6, 1), pltpu.roll(v, 2, 1))
    return jnp.where((row & 1) == 0, pltpu.roll(v, 7, 1), pltpu.roll(v, 1, 1))


def gelu(x):
    return 0.5 * x * (1.0 + jnp.tanh(0.7978845608028654 * (x + 0.044715 * (x * x * x))))


def kernel(ndev, n, field, south, sign, weights, bias, out, wf, wh, wl, slab, xh, xl, gain,
           wsem, lsem, ssem, rsem):
    me = lax.axis_index("lon")
    right, left, twin = lax.rem(me + 1, ndev), lax.rem(me + ndev - 1, ndev), ndev - 1 - me
    total = n + 2 * W

    loads = [pltpu.make_async_copy(weights.at[pl.ds(9 * l, 9)], wf.at[pl.ds(9 * l, 9)], wsem.at[l]) for l in range(4)]
    loads[0].start()
    own = [pltpu.make_async_copy(field, slab.at[0, 0, pl.ds(W, n), pl.ds(8, R)], lsem.at[0]),
           pltpu.make_async_copy(south, slab.at[0, 0, pl.ds(W, n), pl.ds(0, 8)], lsem.at[1])]
    for c in own:
        c.start()
    for c in loads[1:]:
        c.start()

    barrier = pltpu.get_barrier_semaphore()
    for peer in (left, right, twin):
        pl.semaphore_signal(barrier, inc=1, device_id=(peer,), device_id_type=MESH)
    pl.semaphore_wait(barrier, 3)

    def remote(src, dst, k, peer):
        return pltpu.make_async_remote_copy(src_ref=src, dst_ref=dst, send_sem=ssem.at[k], recv_sem=rsem.at[k],
                                            device_id=(peer,), device_id_type=MESH)

    fold = [remote(field.at[:, pl.ds(8, 8)], slab.at[1, 0, pl.ds(W, n), pl.ds(16, 8)], 0, twin),
            remote(field.at[:, pl.ds(0, 8)], slab.at[1, 0, pl.ds(W, n), pl.ds(8, 8)], 1, twin)]
    edge = [remote(field.at[pl.ds(n - W, W)], slab.at[0, 0, pl.ds(0, W), pl.ds(8, R)], 2, right),
            remote(field.at[pl.ds(0, W)], slab.at[0, 0, pl.ds(W + n, W), pl.ds(8, R)], 3, left),
            remote(south.at[pl.ds(n - W, W)], slab.at[0, 0, pl.ds(0, W), pl.ds(0, 8)], 4, right),
            remote(south.at[pl.ds(0, W)], slab.at[0, 0, pl.ds(W + n, W), pl.ds(0, 8)], 5, left)]

    def onward(row, k):
        rows = pl.ds(row, 8)
        return [remote(slab.at[1, 0, pl.ds(n, W), rows], slab.at[1, 0, pl.ds(0, W), rows], k, left),
                remote(slab.at[1, 0, pl.ds(W, W), rows], slab.at[1, 0, pl.ds(W + n, W), rows], k + 1, right)]

    upper, lower = onward(16, 6), onward(8, 8)

    fold[0].start()
    for c in edge:
        c.start()
    fold[1].start()

    def prepare(l):
        loads[l].wait()

        def one(t, _):
            w = wf[t]
            hi = w.astype(BF16)
            wh[t] = hi
            wl[t] = (w - hi.astype(F32)).astype(BF16)
            return 0

        lax.fori_loop(9 * l, 9 * l + 9, one, 0)

    def group(count):
        return 4 if count % 4 == 0 else 3 if count % 3 == 0 else 2

    def north(side, l):
        first = 2 ** l - 1
        count = total - 2 * first
        g = group(count)

        def one(j, _):
            start = first + g * j
            v = slab[1 - side, l, pl.ds(total - g - start, g), pl.ds(16, 8), :]
            v = reverse_rows(v) * sign[...]
            for k in range(g):
                slab[side, l, pl.ds(start + k, 1), pl.ds(24, 8), :] = v[g - 1 - k:g - k]
            return 0

        lax.fori_loop(0, count // g, one, 0)

    def build(l, windows, cols):
        s = 2 ** l
        count = cols + 2 * s
        g = group(count)

        def one(j, _):
            for a in range(3):
                x = jnp.concatenate([slab[side, l, pl.ds(col - s + g * j, g), pl.ds(row + (a - 1) * s, 8), :]
                                     for side, row, col in windows], axis=1)
                hi = x.astype(BF16)
                xh[a, pl.ds(g * j, g)] = hi
                xl[a, pl.ds(g * j, g)] = (x - hi.astype(F32)).astype(BF16)
            return 0

        lax.fori_loop(0, count // g, one, 0)

    def update(l, windows, cols):
        g = group(cols)

        def one(j, _):
            for k, (side, row, col) in enumerate(windows):
                place = pl.ds(col + g * j, g)
                new = slab[side, l, place, pl.ds(row, 8), :] + gain[pl.ds(g * j, g), pl.ds(8 * k, 8), :]
                if l == 3:
                    out[pl.ds(col - W + g * j, g), pl.ds(row - 8, 8), :] = new
                else:
                    slab[side, l + 1, place, pl.ds(row, 8), :] = new
            return 0

        lax.fori_loop(0, cols // g, one, 0)

    def chunk(l, s, start):
        d = None
        for i in range(9):
            a, b = i // 3, i % 3
            rows = pl.ds(start + b * s, PIECE)
            h = xh[a, rows].reshape(PIECE * R, -1)
            lo = xl[a, rows].reshape(PIECE * R, -1)
            for x, w in ((h, wh), (lo, wh), (h, wl)):
                e = jnp.dot(x, w[9 * l + i], preferred_element_type=F32)
                d = e if d is None else d + e
        gain[pl.ds(start, PIECE)] = gelu(d + bias[pl.ds(l, 1)]).reshape(PIECE, R, -1)

    c1, c2, c3 = 1, 3, 7
    n1, n2, n3 = total - 2, total - 6, total - 14
    S8, S16, M16 = (0, 8), (0, 16), (1, 16)

    def pair(x, y, c):
        return [x + (c,), y + (c,)]

    def halves(x, c, m):
        return [x + (c,), x + (c + m // 2,)]

    def start_all(copies):
        for c in copies:
            c.start()

    def wait_all(copies):
        for c in copies:
            c.wait()

    def first():
        wait_all(own)
        wait_all(edge)
        for l in range(1, 4):
            slab[0, l, :, pl.ds(0, 8), :] = slab[0, 0, :, pl.ds(0, 8), :]
            slab[1, l, :, pl.ds(0, 8), :] = zero

    def upper_sent():
        fold[0].wait()
        start_all(upper)

    def upper_here():
        wait_all(upper)
        north(0, 0)
        north(1, 0)

    def lower_sent():
        fold[1].wait()
        start_all(lower)
        north(0, 2)

    def lower_here():
        wait_all(lower)
        north(1, 2)

    steps = [
        (0, pair(S8, S16, c1), n1, first),
        (1, pair(S8, S16, c2), n2, None),
        (2, halves(S8, c3, n3), n3 // 2, upper_sent),
        (0, pair(S16, (1, 17), c1), n1, upper_here),
        (1, pair(S16, M16, c2), n2, lambda: (north(0, 1), north(1, 1))),
        (2, halves(S16, c3, n3), n3 // 2, lower_sent),
        (0, halves((1, 9), c1, n1), n1 // 2, lower_here),
        (1, halves((1, 12), c2, n2), n2 // 2, None),
        (2, halves(M16, c3, n3), n3 // 2, None),
        (3, pair(S8, S16, W), n, lambda: north(0, 3)),
    ]

    zero = jnp.zeros((total, 8, slab.shape[-1]), F32)
    slab[1, 0, :, pl.ds(0, 8), :] = zero
    for l in range(4):
        prepare(l)

    def step(p, _):
        l = jnp.int32(0)
        cols = jnp.int32(0)
        for k, (layer, windows, count, before) in enumerate(steps):
            @pl.when(p == k)
            def _():
                if before is not None:
                    before()
                build(layer, windows, count)

            l = jnp.where(p == k, layer, l)
            cols = jnp.where(p == k, count, cols)
        s = jnp.where(l == 0, 1, jnp.where(l == 1, 2, jnp.where(l == 2, 4, 8)))

        def one(q, _):
            chunk(l, s, jnp.minimum(q * PIECE, cols - PIECE))
            return 0

        lax.fori_loop(0, (cols + PIECE - 1) // PIECE, one, 0)
        for k, (layer, windows, count, before) in enumerate(steps):
            @pl.when(p == k)
            def _():
                update(layer, windows, count)
        return 0

    lax.fori_loop(0, len(steps), step, 0)


def local(ndev, field, south, sign, weights, bias):
    rows, n, c = field.shape
    total = n + 2 * W
    weights = weights.reshape(-1, c, c)
    taps = weights.shape[0]
    any_ = pl.BlockSpec(memory_space=pl.ANY)
    vmem = pl.BlockSpec(memory_space=pltpu.VMEM)
    result = pl.pallas_call(
        functools.partial(kernel, ndev, n),
        out_shape=jax.ShapeDtypeStruct((n, rows, c), F32),
        in_specs=[any_, any_, vmem, any_, vmem],
        out_specs=vmem,
        scratch_shapes=[
            pltpu.VMEM((taps, c, c), F32),
            pltpu.VMEM((taps, c, c), BF16),
            pltpu.VMEM((taps, c, c), BF16),
            pltpu.VMEM((2, 4, total, 32, c), F32),
            pltpu.VMEM((3, total, R, c), BF16),
            pltpu.VMEM((3, total, R, c), BF16),
            pltpu.VMEM((total, R, c), F32),
            pltpu.SemaphoreType.DMA((4,)),
            pltpu.SemaphoreType.DMA((2,)),
            pltpu.SemaphoreType.DMA((10,)),
            pltpu.SemaphoreType.DMA((10,)),
        ],
        compiler_params=pltpu.CompilerParams(collective_id=0, has_side_effects=True, vmem_limit_bytes=60 << 20),
    )(field.transpose(1, 0, 2), south.transpose(1, 0, 2), sign.astype(F32).reshape(1, -1), weights, bias)
    return result.transpose(1, 0, 2)


def solution(mesh):
    ndev = mesh.shape["lon"]
    lon = P(None, "lon", None)
    return jax.shard_map(functools.partial(local, ndev), mesh=mesh, in_specs=(lon, lon, P(), P(), P()),
                         out_specs=lon, check_vma=False)
```

```python
import functools

import jax
import jax.numpy as jnp
from jax import lax
from jax.experimental import pallas as pl
from jax.experimental.pallas import tpu as pltpu
from jax.sharding import PartitionSpec as P

MESH = pl.DeviceIdType.MESH
F32 = jnp.float32
BF16 = jnp.bfloat16
R = 16
PIECE = 20
LANES = 128
W = 15


def reverse_rows(v):
    row = lax.broadcasted_iota(jnp.int32, v.shape, 1)
    v = pltpu.roll(v, 4, 1)
    v = jnp.where((row & 2) == 0, pltpu.roll(v, 6, 1), pltpu.roll(v, 2, 1))
    return jnp.where((row & 1) == 0, pltpu.roll(v, 7, 1), pltpu.roll(v, 1, 1))


def parcels(n, c):
    tail = c - LANES - 64
    share = LANES // tail
    parts, spans, first = [], [], 0
    for columns in (list(range(W)) + list(range(n - W, n)), list(range(W, n - W))):
        half = len(columns) // 2
        pairs = list(zip(columns[:half], columns[half:]))
        rests = [columns[k:k + share] for k in range(0, len(columns), share)]
        count = len(columns) + half + len(rests)
        parts.append((first, columns, pairs, rests))
        spans.append((first, count))
        first += count
    return parts, spans


def gelu(x):
    return 0.5 * x * (1.0 + jnp.tanh(0.7978845608028654 * (x + 0.044715 * (x * x * x))))


def kernel(ndev, n, field, south, sign, weights, bias, out, wf, wh, wl, slab, xh, xl, gain, raw, parcel, landed,
           wsem, lsem, ssem, rsem):
    me = lax.axis_index("lon")
    right, left, twin = lax.rem(me + 1, ndev), lax.rem(me + ndev - 1, ndev), ndev - 1 - me
    total = n + 2 * W

    barrier = pltpu.get_barrier_semaphore()
    for peer in (left, right, twin):
        pl.semaphore_signal(barrier, inc=1, device_id=(peer,), device_id_type=MESH)

    loads = [pltpu.make_async_copy(weights.at[pl.ds(9 * l, 9)], wf.at[pl.ds(9 * l, 9)], wsem.at[l]) for l in range(4)]
    loads[0].start()
    own = [pltpu.make_async_copy(field, slab.at[0, 0, pl.ds(W, n), pl.ds(8, R)], lsem.at[0]),
           pltpu.make_async_copy(south, slab.at[0, 0, pl.ds(W, n), pl.ds(0, 8)], lsem.at[1])]
    for c in own:
        c.start()
    for c in loads[1:]:
        c.start()

    def remote(src, dst, k, peer):
        return pltpu.make_async_remote_copy(src_ref=src, dst_ref=dst, send_sem=ssem.at[k], recv_sem=rsem.at[k],
                                            device_id=(peer,), device_id_type=MESH)

    parts, spans = parcels(n, field.shape[-1])
    tail = field.shape[-1] - LANES - 64

    def pack(half):
        rows = pl.ds(16 - 8 * half, 8)
        lane = lax.broadcasted_iota(jnp.int32, (8, LANES), 1)
        blank = jnp.zeros((8, LANES - 64 - tail), F32)

        def upper_lanes(j):
            return jnp.concatenate([slab[0, 0, W + j, rows, LANES:], blank], axis=1)

        for first, columns, pairs, rests in parts:
            t = first
            for j in columns:
                parcel[half, t] = slab[0, 0, W + j, rows, :LANES]
                t += 1
            for j, k in pairs:
                parcel[half, t] = jnp.where(lane < 64, upper_lanes(j), pltpu.roll(upper_lanes(k), 64, 1))
                t += 1
            for some in rests:
                v = pltpu.roll(upper_lanes(some[0]), 64, 1)
                for k, j in enumerate(some[1:], 1):
                    v = jnp.where(lane < tail * k, v, pltpu.roll(upper_lanes(j), (64 + tail * k) % LANES, 1))
                parcel[half, t] = v
                t += 1

    def unpack(half, part):
        rows = pl.ds(16 - 8 * half, 8)
        lane = lax.broadcasted_iota(jnp.int32, (8, LANES), 1)
        first, columns, pairs, rests = parts[part]
        t = first
        for j in columns:
            slab[1, 0, W + j, rows, :LANES] = landed[half, t]
            t += 1
        wide = {}
        for pair in pairs:
            v = landed[half, t]
            wide[pair[0]], wide[pair[1]] = v, pltpu.roll(v, 64, 1)
            t += 1
        for some in rests:
            v = landed[half, t]
            for k, j in enumerate(some):
                last = pltpu.roll(v, (64 - tail * k) % LANES, 1)
                slab[1, 0, W + j, rows, LANES:] = jnp.where(lane < 64, wide[j], last)[:, :64 + tail]
            t += 1

    def parcel_copy(half, part, k):
        first, count = spans[part]
        place = (half, pl.ds(first, count), pl.ds(half, 8 - half))
        return remote(parcel.at[place], landed.at[place], k, twin)

    fold = [[parcel_copy(half, part, (0, 1, 10, 11)[2 * half + part]) for part in range(2)] for half in range(2)]
    edge = [remote(field.at[pl.ds(n - W, W)], slab.at[0, 0, pl.ds(0, W), pl.ds(8, R)], 2, right),
            remote(field.at[pl.ds(0, W)], slab.at[0, 0, pl.ds(W + n, W), pl.ds(8, R)], 3, left),
            remote(south.at[pl.ds(n - W, W)], slab.at[0, 0, pl.ds(0, W), pl.ds(0, 8)], 4, right),
            remote(south.at[pl.ds(0, W)], slab.at[0, 0, pl.ds(W + n, W), pl.ds(0, 8)], 5, left)]

    def onward(row, k):
        rows = pl.ds(row, 8)
        return [remote(slab.at[1, 0, pl.ds(n, W), rows], slab.at[1, 0, pl.ds(0, W), rows], k, left),
                remote(slab.at[1, 0, pl.ds(W, W), rows], slab.at[1, 0, pl.ds(W + n, W), rows], k + 1, right)]

    upper, lower = onward(16, 6), onward(8, 8)

    own[0].wait()
    pack(0)
    pack(1)
    pl.semaphore_wait(barrier, 3)
    for c in edge:
        c.start()
    for c in fold[0]:
        c.start()
    for c in fold[1]:
        c.start()

    def prepare(l):
        loads[l].wait()

        def one(t, _):
            w = wf[t]
            hi = w.astype(BF16)
            wh[t] = hi
            wl[t] = (w - hi.astype(F32)).astype(BF16)
            return 0

        lax.fori_loop(9 * l, 9 * l + 9, one, 0)

    def group(count):
        return 4 if count % 4 == 0 else 3 if count % 3 == 0 else 2

    def north(side, l):
        first = 2 ** l - 1
        count = total - 2 * first
        g = group(count)

        def one(j, _):
            start = first + g * j
            v = slab[1 - side, l, pl.ds(total - g - start, g), pl.ds(16, 8), :]
            v = reverse_rows(v) * sign[...]
            for k in range(g):
                slab[side, l, pl.ds(start + k, 1), pl.ds(24, 8), :] = v[g - 1 - k:g - k]
            return 0

        lax.fori_loop(0, count // g, one, 0)

    def build(l, windows, cols):
        s = 2 ** l
        count = cols + 2 * s
        g = group(count)

        def one(j, _):
            for a in range(3):
                x = jnp.concatenate([slab[side, l, pl.ds(col - s + g * j, g), pl.ds(row + (a - 1) * s, 8), :]
                                     for side, row, col in windows], axis=1)
                hi = x.astype(BF16)
                xh[a, pl.ds(g * j, g)] = hi
                xl[a, pl.ds(g * j, g)] = (x - hi.astype(F32)).astype(BF16)
            return 0

        lax.fori_loop(0, count // g, one, 0)

    def update(l, windows, cols):
        g = group(cols)

        def one(j, _):
            for k, (side, row, col) in enumerate(windows):
                place = pl.ds(col + g * j, g)
                new = slab[side, l, place, pl.ds(row, 8), :] + gain[pl.ds(g * j, g), pl.ds(8 * k, 8), :]
                if l == 3:
                    out[pl.ds(col - W + g * j, g), pl.ds(row - 8, 8), :] = new
                else:
                    slab[side, l + 1, place, pl.ds(row, 8), :] = new
            return 0

        lax.fori_loop(0, cols // g, one, 0)

    def chunk(l, s, start, slot):
        d = None
        for i in range(9):
            a, b = i // 3, i % 3
            rows = pl.ds(start + b * s, PIECE)
            h = xh[a, rows].reshape(PIECE * R, -1)
            lo = xl[a, rows].reshape(PIECE * R, -1)
            for x, w in ((h, wh), (lo, wh), (h, wl)):
                e = jnp.dot(x, w[9 * l + i], preferred_element_type=F32)
                d = e if d is None else d + e
        raw[slot] = d

    def finish(l, start, slot):
        gain[pl.ds(start, PIECE)] = gelu(raw[slot] + bias[pl.ds(l, 1)]).reshape(PIECE, R, -1)

    c1, c2, c3 = 1, 3, 7
    n1, n2, n3 = total - 2, total - 6, total - 14
    S8, S16, M16 = (0, 8), (0, 16), (1, 16)

    def pair(x, y, c):
        return [x + (c,), y + (c,)]

    def halves(x, c, m):
        return [x + (c,), x + (c + m // 2,)]

    def start_all(copies):
        for c in copies:
            c.start()

    def wait_all(copies):
        for c in copies:
            c.wait()

    def first():
        own[1].wait()
        wait_all(edge)
        for l in range(1, 4):
            slab[0, l, :, pl.ds(0, 8), :] = slab[0, 0, :, pl.ds(0, 8), :]
            slab[1, l, :, pl.ds(0, 8), :] = zero

    def upper_sent():
        fold[0][0].wait()
        unpack(0, 0)
        start_all(upper)

    def upper_here():
        fold[0][1].wait()
        unpack(0, 1)
        wait_all(upper)
        north(0, 0)
        north(1, 0)

    def lower_sent():
        fold[1][0].wait()
        unpack(1, 0)
        start_all(lower)
        north(0, 2)

    def lower_here():
        fold[1][1].wait()
        unpack(1, 1)
        wait_all(lower)
        north(1, 2)

    steps = [
        (0, pair(S8, S16, c1), n1, first),
        (1, pair(S8, S16, c2), n2, None),
        (2, halves(S8, c3, n3), n3 // 2, upper_sent),
        (0, pair(S16, (1, 17), c1), n1, upper_here),
        (1, pair(S16, M16, c2), n2, lambda: (north(0, 1), north(1, 1))),
        (2, halves(S16, c3, n3), n3 // 2, lower_sent),
        (0, halves((1, 9), c1, n1), n1 // 2, lower_here),
        (1, halves((1, 12), c2, n2), n2 // 2, None),
        (2, halves(M16, c3, n3), n3 // 2, None),
        (3, pair(S8, S16, W), n, lambda: north(0, 3)),
    ]

    zero = jnp.zeros((total, 8, slab.shape[-1]), F32)
    slab[1, 0, :, pl.ds(0, 8), :] = zero
    for l in range(4):
        prepare(l)

    def step(p, _):
        l = jnp.int32(0)
        cols = jnp.int32(0)
        for k, (layer, windows, count, before) in enumerate(steps):
            @pl.when(p == k)
            def _():
                if before is not None:
                    before()
                build(layer, windows, count)

            l = jnp.where(p == k, layer, l)
            cols = jnp.where(p == k, count, cols)
        s = jnp.where(l == 0, 1, jnp.where(l == 1, 2, jnp.where(l == 2, 4, 8)))

        pieces = (cols + PIECE - 1) // PIECE

        def place(q):
            return jnp.maximum(jnp.minimum(q * PIECE, cols - PIECE), 0)

        def one(q, _):
            finish(l, place(q - 1), (q + 1) % 2)
            chunk(l, s, place(q), q % 2)
            return 0

        lax.fori_loop(0, pieces, one, 0)
        finish(l, place(pieces - 1), (pieces + 1) % 2)
        for k, (layer, windows, count, before) in enumerate(steps):
            @pl.when(p == k)
            def _():
                update(layer, windows, count)
        return 0

    lax.fori_loop(0, len(steps), step, 0)


def local(ndev, field, south, sign, weights, bias):
    rows, n, c = field.shape
    total = n + 2 * W
    weights = weights.reshape(-1, c, c)
    tiles = sum(count for _, count in parcels(n, c)[1])
    taps = weights.shape[0]
    any_ = pl.BlockSpec(memory_space=pl.ANY)
    vmem = pl.BlockSpec(memory_space=pltpu.VMEM)
    result = pl.pallas_call(
        functools.partial(kernel, ndev, n),
        out_shape=jax.ShapeDtypeStruct((n, rows, c), F32),
        in_specs=[any_, any_, vmem, any_, vmem],
        out_specs=vmem,
        scratch_shapes=[
            pltpu.VMEM((taps, c, c), F32),
            pltpu.VMEM((taps, c, c), BF16),
            pltpu.VMEM((taps, c, c), BF16),
            pltpu.VMEM((2, 4, total, 32, c), F32),
            pltpu.VMEM((3, total, R, c), BF16),
            pltpu.VMEM((3, total, R, c), BF16),
            pltpu.VMEM((total, R, c), F32),
            pltpu.VMEM((2, PIECE * R, c), F32),
            pltpu.VMEM((2, tiles, 8, LANES), F32),
            pltpu.VMEM((2, tiles, 8, LANES), F32),
            pltpu.SemaphoreType.DMA((4,)),
            pltpu.SemaphoreType.DMA((2,)),
            pltpu.SemaphoreType.DMA((12,)),
            pltpu.SemaphoreType.DMA((12,)),
        ],
        compiler_params=pltpu.CompilerParams(collective_id=0, has_side_effects=True, vmem_limit_bytes=60 << 20),
    )(field.transpose(1, 0, 2), south.transpose(1, 0, 2), sign.astype(F32).reshape(1, -1), weights, bias)
    return result.transpose(1, 0, 2)


def solution(mesh):
    ndev = mesh.shape["lon"]
    lon = P(None, "lon", None)
    return jax.shard_map(functools.partial(local, ndev), mesh=mesh, in_specs=(lon, lon, P(), P(), P()),
                         out_specs=lon, check_vma=False)
```

```python
import functools

import jax
import jax.numpy as jnp
from jax import lax
from jax.experimental import pallas as pl
from jax.experimental.pallas import tpu as pltpu
from jax.sharding import PartitionSpec as P

MESH = pl.DeviceIdType.MESH
F32 = jnp.float32
BF16 = jnp.bfloat16
R = 16
MOST = 4
PIECE = 20
LANES = 128
W = 15


def reverse_rows(v):
    row = lax.broadcasted_iota(jnp.int32, v.shape, 1)
    v = pltpu.roll(v, 4, 1)
    v = jnp.where((row & 2) == 0, pltpu.roll(v, 6, 1), pltpu.roll(v, 2, 1))
    return jnp.where((row & 1) == 0, pltpu.roll(v, 7, 1), pltpu.roll(v, 1, 1))


def parcels(n, c):
    tail = c - LANES - 64
    share = LANES // tail
    parts, spans, first = [], [], 0
    for columns in (list(range(W)) + list(range(n - W, n)), list(range(W, n - W))):
        half = len(columns) // 2
        pairs = list(zip(columns[:half], columns[half:]))
        rests = [columns[k:k + share] for k in range(0, len(columns), share)]
        count = len(columns) + half + len(rests)
        parts.append((first, columns, pairs, rests))
        spans.append((first, count))
        first += count
    return parts, spans


def gelu(x):
    return 0.5 * x * (1.0 + jnp.tanh(0.7978845608028654 * (x + 0.044715 * (x * x * x))))


def kernel(ndev, n, field, south, sign, weights, bias, out, wf, wh, wl, slab, xh, xl, gain, raw, parcel, landed,
           wsem, lsem, ssem, rsem):
    me = lax.axis_index("lon")
    right, left, twin = lax.rem(me + 1, ndev), lax.rem(me + ndev - 1, ndev), ndev - 1 - me
    total = n + 2 * W

    barrier = pltpu.get_barrier_semaphore()
    for peer in (left, right, twin):
        pl.semaphore_signal(barrier, inc=1, device_id=(peer,), device_id_type=MESH)

    loads = [pltpu.make_async_copy(weights.at[pl.ds(9 * l, 9)], wf.at[pl.ds(9 * l, 9)], wsem.at[l]) for l in range(4)]
    loads[0].start()
    own = [pltpu.make_async_copy(field, slab.at[0, 0, pl.ds(W, n), pl.ds(8, R)], lsem.at[0]),
           pltpu.make_async_copy(south, slab.at[0, 0, pl.ds(W, n), pl.ds(0, 8)], lsem.at[1])]
    for c in own:
        c.start()
    for c in loads[1:]:
        c.start()

    def remote(src, dst, k, peer):
        return pltpu.make_async_remote_copy(src_ref=src, dst_ref=dst, send_sem=ssem.at[k], recv_sem=rsem.at[k],
                                            device_id=(peer,), device_id_type=MESH)

    parts, spans = parcels(n, field.shape[-1])
    tail = field.shape[-1] - LANES - 64

    def pack(half):
        rows = pl.ds(16 - 8 * half, 8)
        lane = lax.broadcasted_iota(jnp.int32, (8, LANES), 1)
        blank = jnp.zeros((8, LANES - 64 - tail), F32)

        def upper_lanes(j):
            return jnp.concatenate([slab[0, 0, W + j, rows, LANES:], blank], axis=1)

        for first, columns, pairs, rests in parts:
            t = first
            for j in columns:
                parcel[half, t] = slab[0, 0, W + j, rows, :LANES]
                t += 1
            for j, k in pairs:
                parcel[half, t] = jnp.where(lane < 64, upper_lanes(j), pltpu.roll(upper_lanes(k), 64, 1))
                t += 1
            for some in rests:
                v = pltpu.roll(upper_lanes(some[0]), 64, 1)
                for k, j in enumerate(some[1:], 1):
                    v = jnp.where(lane < tail * k, v, pltpu.roll(upper_lanes(j), (64 + tail * k) % LANES, 1))
                parcel[half, t] = v
                t += 1

    def unpack(half, part):
        rows = pl.ds(16 - 8 * half, 8)
        lane = lax.broadcasted_iota(jnp.int32, (8, LANES), 1)
        first, columns, pairs, rests = parts[part]
        t = first
        for j in columns:
            slab[1, 0, W + j, rows, :LANES] = landed[half, t]
            t += 1
        wide = {}
        for pair in pairs:
            v = landed[half, t]
            wide[pair[0]], wide[pair[1]] = v, pltpu.roll(v, 64, 1)
            t += 1
        for some in rests:
            v = landed[half, t]
            for k, j in enumerate(some):
                last = pltpu.roll(v, (64 - tail * k) % LANES, 1)
                slab[1, 0, W + j, rows, LANES:] = jnp.where(lane < 64, wide[j], last)[:, :64 + tail]
            t += 1

    def parcel_copy(half, part, k):
        first, count = spans[part]
        place = (half, pl.ds(first, count), pl.ds(half, 8 - half))
        return remote(parcel.at[place], landed.at[place], k, twin)

    fold = [[parcel_copy(half, part, (0, 1, 10, 11)[2 * half + part]) for part in range(2)] for half in range(2)]
    edge = [remote(field.at[pl.ds(n - W, W)], slab.at[0, 0, pl.ds(0, W), pl.ds(8, R)], 2, right),
            remote(field.at[pl.ds(0, W)], slab.at[0, 0, pl.ds(W + n, W), pl.ds(8, R)], 3, left),
            remote(south.at[pl.ds(n - W, W)], slab.at[0, 0, pl.ds(0, W), pl.ds(0, 8)], 4, right),
            remote(south.at[pl.ds(0, W)], slab.at[0, 0, pl.ds(W + n, W), pl.ds(0, 8)], 5, left)]

    def onward(row, k):
        rows = pl.ds(row, 8)
        return [remote(slab.at[1, 0, pl.ds(n, W), rows], slab.at[1, 0, pl.ds(0, W), rows], k, left),
                remote(slab.at[1, 0, pl.ds(W, W), rows], slab.at[1, 0, pl.ds(W + n, W), rows], k + 1, right)]

    upper, lower = onward(16, 6), onward(8, 8)

    own[0].wait()
    pack(0)
    pack(1)
    pl.semaphore_wait(barrier, 3)
    for c in edge:
        c.start()
    for c in fold[0]:
        c.start()

    def prepare(l):
        loads[l].wait()

        def one(t, _):
            w = wf[t]
            hi = w.astype(BF16)
            wh[t] = hi
            wl[t] = (w - hi.astype(F32)).astype(BF16)
            return 0

        lax.fori_loop(9 * l, 9 * l + 9, one, 0)

    def group(count):
        return max(g for g in range(1, MOST + 1) if count % g == 0)

    def north(side, l):
        first = 2 ** l - 1
        count = total - 2 * first
        g = group(count)

        def one(j, _):
            start = first + g * j
            v = slab[1 - side, l, pl.ds(total - g - start, g), pl.ds(16, 8), :]
            v = reverse_rows(v) * sign[...]
            for k in range(g):
                slab[side, l, pl.ds(start + k, 1), pl.ds(24, 8), :] = v[g - 1 - k:g - k]
            return 0

        lax.fori_loop(0, count // g, one, 0)

    def build(l, windows, cols, at):
        s = 2 ** l
        count = cols + 2 * s
        g = group(count)

        def one(j, _):
            for a in range(3):
                x = jnp.concatenate([slab[side, l, pl.ds(col - s + g * j, g), pl.ds(row + (a - 1) * s, 8), :]
                                     for side, row, col in windows], axis=1)
                hi = x.astype(BF16)
                xh[a, pl.ds(at + g * j, g)] = hi
                xl[a, pl.ds(at + g * j, g)] = (x - hi.astype(F32)).astype(BF16)
            return 0

        lax.fori_loop(0, count // g, one, 0)

    def update(l, windows, cols, at):
        g = group(cols)

        def one(j, _):
            for k, (side, row, col) in enumerate(windows):
                place = pl.ds(col + g * j, g)
                new = slab[side, l, place, pl.ds(row, 8), :] + gain[pl.ds(at + g * j, g), pl.ds(8 * k, 8), :]
                if l == 3:
                    out[pl.ds(col - W + g * j, g), pl.ds(row - 8, 8), :] = new
                else:
                    slab[side, l + 1, place, pl.ds(row, 8), :] = new
            return 0

        lax.fori_loop(0, cols // g, one, 0)

    def chunk(l, s, start, slot):
        d = None
        for i in range(9):
            a, b = i // 3, i % 3
            rows = pl.ds(start + b * s, PIECE)
            h = xh[a, rows].reshape(PIECE * R, -1)
            lo = xl[a, rows].reshape(PIECE * R, -1)
            for x, w in ((h, wh), (lo, wh), (h, wl)):
                e = jnp.dot(x, w[9 * l + i], preferred_element_type=F32)
                d = e if d is None else d + e
        raw[slot] = d

    def finish(l, start, slot):
        gain[pl.ds(start, PIECE)] = gelu(raw[slot] + bias[pl.ds(l, 1)]).reshape(PIECE, R, -1)

    c1, c2, c3 = 1, 3, 7
    n1, n2, n3 = total - 2, total - 6, total - 14
    S8, S16, M16 = (0, 8), (0, 16), (1, 16)

    def pair(x, y, c):
        return [x + (c,), y + (c,)]

    def halves(x, c, m):
        return [x + (c,), x + (c + m // 2,)]

    def start_all(copies):
        for c in copies:
            c.start()

    def wait_all(copies):
        for c in copies:
            c.wait()

    def south_rows(cols):
        for l in range(1, 4):
            slab[0, l, cols, pl.ds(0, 8), :] = slab[0, 0, cols, pl.ds(0, 8), :]

    def first():
        own[1].wait()
        south_rows(pl.ds(W, n))
        for l in range(1, 4):
            slab[1, l, :, pl.ds(0, 8), :] = zero

    def halo_here():
        wait_all(edge)
        south_rows(pl.ds(0, W))
        south_rows(pl.ds(W + n, W))

    def upper_sent():
        fold[0][0].wait()
        unpack(0, 0)
        start_all(upper)
        start_all(fold[1])

    def upper_here():
        fold[0][1].wait()
        unpack(0, 1)
        wait_all(upper)
        north(0, 0)
        north(1, 0)

    def lower_sent():
        fold[1][0].wait()
        unpack(1, 0)
        start_all(lower)
        north(0, 2)

    def lower_here():
        fold[1][1].wait()
        unpack(1, 1)
        wait_all(lower)
        north(1, 2)

    def split(layer, c, m):
        middle = n - 2 * c
        return ([(pair(S8, S16, W + c), middle)],
                [(pair(S8, S16, c), W), (pair(S8, S16, W + c + middle), W)])

    middle0, sides0 = split(0, c1, n1)
    middle1, sides1 = split(1, c2, n2)
    steps = [
        (0, middle0, first),
        (1, middle1, None),
        (0, sides0, halo_here),
        (1, sides1, None),
        (2, [(halves(S8, c3, n3), n3 // 2)], upper_sent),
        (0, [(pair(S16, (1, 17), c1), n1)], upper_here),
        (1, [(pair(S16, M16, c2), n2)], lambda: (north(0, 1), north(1, 1))),
        (2, [(halves(S16, c3, n3), n3 // 2)], lower_sent),
        (0, [(halves((1, 9), c1, n1), n1 // 2)], lower_here),
        (1, [(halves((1, 12), c2, n2), n2 // 2)], None),
        (2, [(halves(M16, c3, n3), n3 // 2)], None),
        (3, [(pair(S8, S16, W), n)], lambda: north(0, 3)),
    ]

    def placed(layer, segments):
        at, result = 0, []
        for windows, count in segments:
            result.append((windows, count, at))
            at += count + 2 ** (layer + 1)
        return result, at - 2 ** (layer + 1)

    zero = jnp.zeros((total, 8, slab.shape[-1]), F32)
    slab[1, 0, :, pl.ds(0, 8), :] = zero
    for l in range(4):
        prepare(l)

    def step(p, _):
        l = jnp.int32(0)
        cols = jnp.int32(0)
        for k, (layer, segments, before) in enumerate(steps):
            @pl.when(p == k)
            def _():
                if before is not None:
                    before()
                for segment in placed(layer, segments)[0]:
                    build(layer, *segment)

            l = jnp.where(p == k, layer, l)
            cols = jnp.where(p == k, placed(layer, segments)[1], cols)
        s = jnp.where(l == 0, 1, jnp.where(l == 1, 2, jnp.where(l == 2, 4, 8)))

        pieces = (cols + PIECE - 1) // PIECE

        def place(q):
            return jnp.maximum(jnp.minimum(q * PIECE, cols - PIECE), 0)

        def one(q, _):
            finish(l, place(q - 1), (q + 1) % 2)
            chunk(l, s, place(q), q % 2)
            return 0

        lax.fori_loop(0, pieces, one, 0)
        finish(l, place(pieces - 1), (pieces + 1) % 2)
        for k, (layer, segments, before) in enumerate(steps):
            @pl.when(p == k)
            def _():
                for segment in placed(layer, segments)[0]:
                    update(layer, *segment)
        return 0

    lax.fori_loop(0, len(steps), step, 0)


def local(ndev, field, south, sign, weights, bias):
    rows, n, c = field.shape
    total = n + 2 * W
    weights = weights.reshape(-1, c, c)
    tiles = sum(count for _, count in parcels(n, c)[1])
    taps = weights.shape[0]
    any_ = pl.BlockSpec(memory_space=pl.ANY)
    vmem = pl.BlockSpec(memory_space=pltpu.VMEM)
    result = pl.pallas_call(
        functools.partial(kernel, ndev, n),
        out_shape=jax.ShapeDtypeStruct((n, rows, c), F32),
        in_specs=[any_, any_, vmem, any_, vmem],
        out_specs=vmem,
        scratch_shapes=[
            pltpu.VMEM((taps, c, c), F32),
            pltpu.VMEM((taps, c, c), BF16),
            pltpu.VMEM((taps, c, c), BF16),
            pltpu.VMEM((2, 4, total, 32, c), F32),
            pltpu.VMEM((3, total, R, c), BF16),
            pltpu.VMEM((3, total, R, c), BF16),
            pltpu.VMEM((total, R, c), F32),
            pltpu.VMEM((2, PIECE * R, c), F32),
            pltpu.VMEM((2, tiles, 8, LANES), F32),
            pltpu.VMEM((2, tiles, 8, LANES), F32),
            pltpu.SemaphoreType.DMA((4,)),
            pltpu.SemaphoreType.DMA((2,)),
            pltpu.SemaphoreType.DMA((12,)),
            pltpu.SemaphoreType.DMA((12,)),
        ],
        compiler_params=pltpu.CompilerParams(collective_id=0, has_side_effects=True, vmem_limit_bytes=60 << 20),
    )(field.transpose(1, 0, 2), south.transpose(1, 0, 2), sign.astype(F32).reshape(1, -1), weights, bias)
    return result.transpose(1, 0, 2)


def solution(mesh):
    ndev = mesh.shape["lon"]
    lon = P(None, "lon", None)
    return jax.shard_map(functools.partial(local, ndev), mesh=mesh, in_specs=(lon, lon, P(), P(), P()),
                         out_specs=lon, check_vma=False)
```

```python
import functools

import jax
import jax.numpy as jnp
from jax import lax
from jax.experimental import pallas as pl
from jax.experimental.pallas import tpu as pltpu
from jax.sharding import PartitionSpec as P

MESH = pl.DeviceIdType.MESH
F32 = jnp.float32
BF16 = jnp.bfloat16
R = 16
MOST = 8
PIECES = (20, 19, 17, 26)
LANES = 128
W = 15


def reverse_rows(v):
    row = lax.broadcasted_iota(jnp.int32, v.shape, 1)
    v = pltpu.roll(v, 4, 1)
    v = jnp.where((row & 2) == 0, pltpu.roll(v, 6, 1), pltpu.roll(v, 2, 1))
    return jnp.where((row & 1) == 0, pltpu.roll(v, 7, 1), pltpu.roll(v, 1, 1))


def parcels(n, c):
    tail = c - LANES - 64
    share = LANES // tail
    parts, spans, first = [], [], 0
    for columns in (list(range(W)) + list(range(n - W, n)), list(range(W, n - W))):
        half = len(columns) // 2
        pairs = list(zip(columns[:half], columns[half:]))
        rests = [columns[k:k + share] for k in range(0, len(columns), share)]
        count = len(columns) + half + len(rests)
        parts.append((first, columns, pairs, rests))
        spans.append((first, count))
        first += count
    return parts, spans


def gelu(x):
    return 0.5 * x * (1.0 + jnp.tanh(0.7978845608028654 * (x + 0.044715 * (x * x * x))))


def kernel(ndev, n, field, south, sign, weights, bias, out, wf, wh, wl, slab, xh, xl, gain, raw, parcel, landed,
           wsem, lsem, ssem, rsem):
    me = lax.axis_index("lon")
    right, left, twin = lax.rem(me + 1, ndev), lax.rem(me + ndev - 1, ndev), ndev - 1 - me
    total = n + 2 * W

    barrier = pltpu.get_barrier_semaphore()
    for peer in (left, right, twin):
        pl.semaphore_signal(barrier, inc=1, device_id=(peer,), device_id_type=MESH)

    loads = [pltpu.make_async_copy(weights.at[pl.ds(9 * l, 9)], wf.at[pl.ds(9 * l, 9)], wsem.at[l]) for l in range(4)]
    loads[0].start()
    own = [pltpu.make_async_copy(field, slab.at[0, 0, pl.ds(W, n), pl.ds(8, R)], lsem.at[0]),
           pltpu.make_async_copy(south, slab.at[0, 0, pl.ds(W, n), pl.ds(0, 8)], lsem.at[1])]
    for c in own:
        c.start()
    for c in loads[1:]:
        c.start()

    def remote(src, dst, k, peer):
        return pltpu.make_async_remote_copy(src_ref=src, dst_ref=dst, send_sem=ssem.at[k], recv_sem=rsem.at[k],
                                            device_id=(peer,), device_id_type=MESH)

    parts, spans = parcels(n, field.shape[-1])
    tail = field.shape[-1] - LANES - 64

    def pack(half):
        rows = pl.ds(16 - 8 * half, 8)
        lane = lax.broadcasted_iota(jnp.int32, (8, LANES), 1)
        blank = jnp.zeros((8, LANES - 64 - tail), F32)

        def upper_lanes(j):
            return jnp.concatenate([slab[0, 0, W + j, rows, LANES:], blank], axis=1)

        for first, columns, pairs, rests in parts:
            t = first
            for j in columns:
                parcel[half, t] = slab[0, 0, W + j, rows, :LANES]
                t += 1
            for j, k in pairs:
                parcel[half, t] = jnp.where(lane < 64, upper_lanes(j), pltpu.roll(upper_lanes(k), 64, 1))
                t += 1
            for some in rests:
                v = pltpu.roll(upper_lanes(some[0]), 64, 1)
                for k, j in enumerate(some[1:], 1):
                    v = jnp.where(lane < tail * k, v, pltpu.roll(upper_lanes(j), (64 + tail * k) % LANES, 1))
                parcel[half, t] = v
                t += 1

    def unpack(half, part):
        rows = pl.ds(16 - 8 * half, 8)
        lane = lax.broadcasted_iota(jnp.int32, (8, LANES), 1)
        first, columns, pairs, rests = parts[part]
        t = first
        for j in columns:
            slab[1, 0, W + j, rows, :LANES] = landed[half, t]
            t += 1
        wide = {}
        for pair in pairs:
            v = landed[half, t]
            wide[pair[0]], wide[pair[1]] = v, pltpu.roll(v, 64, 1)
            t += 1
        for some in rests:
            v = landed[half, t]
            for k, j in enumerate(some):
                last = pltpu.roll(v, (64 - tail * k) % LANES, 1)
                slab[1, 0, W + j, rows, LANES:] = jnp.where(lane < 64, wide[j], last)[:, :64 + tail]
            t += 1

    def parcel_copy(half, part, k):
        first, count = spans[part]
        place = (half, pl.ds(first, count), pl.ds(half, 8 - half))
        return remote(parcel.at[place], landed.at[place], k, twin)

    fold = [[parcel_copy(half, part, (0, 1, 10, 11)[2 * half + part]) for part in range(2)] for half in range(2)]
    edge = [remote(field.at[pl.ds(n - W, W)], slab.at[0, 0, pl.ds(0, W), pl.ds(8, R)], 2, right),
            remote(field.at[pl.ds(0, W)], slab.at[0, 0, pl.ds(W + n, W), pl.ds(8, R)], 3, left),
            remote(south.at[pl.ds(n - W, W)], slab.at[0, 0, pl.ds(0, W), pl.ds(0, 8)], 4, right),
            remote(south.at[pl.ds(0, W)], slab.at[0, 0, pl.ds(W + n, W), pl.ds(0, 8)], 5, left)]

    def onward(row, k):
        rows = pl.ds(row, 8)
        return [remote(slab.at[1, 0, pl.ds(n, W), rows], slab.at[1, 0, pl.ds(0, W), rows], k, left),
                remote(slab.at[1, 0, pl.ds(W, W), rows], slab.at[1, 0, pl.ds(W + n, W), rows], k + 1, right)]

    upper, lower = onward(16, 6), onward(8, 8)

    own[0].wait()
    pack(0)
    pack(1)
    pl.semaphore_wait(barrier, 3)
    for c in edge:
        c.start()
    for c in fold[0]:
        c.start()

    def prepare(l):
        loads[l].wait()

        def one(t, _):
            w = wf[t]
            hi = w.astype(BF16)
            wh[t] = hi
            wl[t] = (w - hi.astype(F32)).astype(BF16)
            return 0

        lax.fori_loop(9 * l, 9 * l + 9, one, 0)

    def group(count):
        return max(g for g in range(1, MOST + 1) if count % g == 0)

    def north(side, l):
        first = 2 ** l - 1
        count = total - 2 * first
        g = group(count)

        def one(j, _):
            start = first + g * j
            v = slab[1 - side, l, pl.ds(total - g - start, g), pl.ds(16, 8), :]
            v = reverse_rows(v) * sign[...]
            for k in range(g):
                slab[side, l, pl.ds(start + k, 1), pl.ds(24, 8), :] = v[g - 1 - k:g - k]
            return 0

        lax.fori_loop(0, count // g, one, 0)

    def build(l, windows, cols, at):
        s = 2 ** l
        count = cols + 2 * s
        g = group(count)

        def one(j, _):
            for a in range(3):
                x = jnp.concatenate([slab[side, l, pl.ds(col - s + g * j, g), pl.ds(row + (a - 1) * s, 8), :]
                                     for side, row, col in windows], axis=1)
                hi = x.astype(BF16)
                xh[a, pl.ds(at + g * j, g)] = hi
                xl[a, pl.ds(at + g * j, g)] = (x - hi.astype(F32)).astype(BF16)
            return 0

        lax.fori_loop(0, count // g, one, 0)

    def update(l, windows, cols, at):
        g = group(cols)

        def one(j, _):
            for k, (side, row, col) in enumerate(windows):
                place = pl.ds(col + g * j, g)
                new = slab[side, l, place, pl.ds(row, 8), :] + gain[pl.ds(at + g * j, g), pl.ds(8 * k, 8), :]
                if l == 3:
                    out[pl.ds(col - W + g * j, g), pl.ds(row - 8, 8), :] = new
                else:
                    slab[side, l + 1, place, pl.ds(row, 8), :] = new
            return 0

        lax.fori_loop(0, cols // g, one, 0)

    def products(l, start, slot):
        s, piece = 2 ** l, PIECES[l]
        d = None
        for i in range(9):
            a, b = i // 3, i % 3
            rows = pl.ds(start + b * s, piece)
            h = xh[a, rows].reshape(piece * R, -1)
            lo = xl[a, rows].reshape(piece * R, -1)
            for x, w in ((h, wh), (lo, wh), (h, wl)):
                e = jnp.dot(x, w[9 * l + i], preferred_element_type=F32)
                d = e if d is None else d + e
        raw[slot, pl.ds(0, piece * R)] = d

    def finish(l, start, slot):
        piece = PIECES[l]
        g = gelu(raw[slot, pl.ds(0, piece * R)] + bias[pl.ds(l, 1)])
        gain[pl.ds(start, piece)] = g.reshape(piece, R, -1)

    def convolve(l, cols):
        piece = PIECES[l]
        pieces = (cols + piece - 1) // piece

        def place(q):
            return jnp.maximum(jnp.minimum(q * piece, cols - piece), 0)

        def one(q, _):
            finish(l, place(q - 1), (q + 1) % 2)
            products(l, place(q), q % 2)
            return 0

        lax.fori_loop(0, pieces, one, 0)
        finish(l, place(pieces - 1), (pieces + 1) % 2)

    c1, c2, c3 = 1, 3, 7
    n1, n2, n3 = total - 2, total - 6, total - 14
    S8, S16, M16 = (0, 8), (0, 16), (1, 16)

    def pair(x, y, c):
        return [x + (c,), y + (c,)]

    def halves(x, c, m):
        return [x + (c,), x + (c + m // 2,)]

    def start_all(copies):
        for c in copies:
            c.start()

    def wait_all(copies):
        for c in copies:
            c.wait()

    def south_rows(cols):
        for l in range(1, 4):
            slab[0, l, cols, pl.ds(0, 8), :] = slab[0, 0, cols, pl.ds(0, 8), :]

    def first():
        own[1].wait()
        south_rows(pl.ds(W, n))
        for l in range(1, 4):
            slab[1, l, :, pl.ds(0, 8), :] = zero

    def halo_here():
        wait_all(edge)
        south_rows(pl.ds(0, W))
        south_rows(pl.ds(W + n, W))

    def upper_sent():
        fold[0][0].wait()
        unpack(0, 0)
        start_all(upper)
        start_all(fold[1])

    def upper_here():
        fold[0][1].wait()
        unpack(0, 1)
        wait_all(upper)
        north(0, 0)
        north(1, 0)

    def lower_sent():
        fold[1][0].wait()
        unpack(1, 0)
        start_all(lower)
        north(0, 2)

    def lower_here():
        fold[1][1].wait()
        unpack(1, 1)
        wait_all(lower)
        north(1, 2)

    def split(layer, c, m):
        middle = n - 2 * c
        return ([(pair(S8, S16, W + c), middle)],
                [(pair(S8, S16, c), W), (pair(S8, S16, W + c + middle), W)])

    middle0, sides0 = split(0, c1, n1)
    middle1, sides1 = split(1, c2, n2)
    steps = [
        (0, middle0, first),
        (1, middle1, None),
        (0, sides0, halo_here),
        (1, sides1, None),
        (2, [(halves(S8, c3, n3), n3 // 2)], upper_sent),
        (0, [(pair(S16, (1, 17), c1), n1)], upper_here),
        (1, [(pair(S16, M16, c2), n2)], lambda: (north(0, 1), north(1, 1))),
        (2, [(halves(S16, c3, n3), n3 // 2)], lower_sent),
        (0, [(halves((1, 9), c1, n1), n1 // 2)], lower_here),
        (1, [(halves((1, 12), c2, n2), n2 // 2)], None),
        (2, [(halves(M16, c3, n3), n3 // 2)], None),
        (3, [(pair(S8, S16, W), n)], lambda: north(0, 3)),
    ]

    def placed(layer, segments):
        at, result = 0, []
        for windows, count in segments:
            result.append((windows, count, at))
            at += count + 2 ** (layer + 1)
        return result, at - 2 ** (layer + 1)

    zero = jnp.zeros((total, 8, slab.shape[-1]), F32)
    slab[1, 0, :, pl.ds(0, 8), :] = zero
    for l in range(4):
        prepare(l)

    def step(p, _):
        l = jnp.int32(0)
        cols = jnp.int32(0)
        for k, (layer, segments, before) in enumerate(steps):
            @pl.when(p == k)
            def _():
                if before is not None:
                    before()
                for segment in placed(layer, segments)[0]:
                    build(layer, *segment)

            l = jnp.where(p == k, layer, l)
            cols = jnp.where(p == k, placed(layer, segments)[1], cols)
        for layer in range(4):
            @pl.when(l == layer)
            def _():
                convolve(layer, cols)
        for k, (layer, segments, before) in enumerate(steps):
            @pl.when(p == k)
            def _():
                for segment in placed(layer, segments)[0]:
                    update(layer, *segment)
        return 0

    lax.fori_loop(0, len(steps), step, 0)


def local(ndev, field, south, sign, weights, bias):
    rows, n, c = field.shape
    total = n + 2 * W
    weights = weights.reshape(-1, c, c)
    tiles = sum(count for _, count in parcels(n, c)[1])
    taps = weights.shape[0]
    any_ = pl.BlockSpec(memory_space=pl.ANY)
    vmem = pl.BlockSpec(memory_space=pltpu.VMEM)
    result = pl.pallas_call(
        functools.partial(kernel, ndev, n),
        out_shape=jax.ShapeDtypeStruct((n, rows, c), F32),
        in_specs=[any_, any_, vmem, any_, vmem],
        out_specs=vmem,
        scratch_shapes=[
            pltpu.VMEM((taps, c, c), F32),
            pltpu.VMEM((taps, c, c), BF16),
            pltpu.VMEM((taps, c, c), BF16),
            pltpu.VMEM((2, 4, total, 32, c), F32),
            pltpu.VMEM((3, total, R, c), BF16),
            pltpu.VMEM((3, total, R, c), BF16),
            pltpu.VMEM((total, R, c), F32),
            pltpu.VMEM((2, max(PIECES) * R, c), F32),
            pltpu.VMEM((2, tiles, 8, LANES), F32),
            pltpu.VMEM((2, tiles, 8, LANES), F32),
            pltpu.SemaphoreType.DMA((4,)),
            pltpu.SemaphoreType.DMA((2,)),
            pltpu.SemaphoreType.DMA((12,)),
            pltpu.SemaphoreType.DMA((12,)),
        ],
        compiler_params=pltpu.CompilerParams(collective_id=0, has_side_effects=True, vmem_limit_bytes=60 << 20),
    )(field.transpose(1, 0, 2), south.transpose(1, 0, 2), sign.astype(F32).reshape(1, -1), weights, bias)
    return result.transpose(1, 0, 2)


def solution(mesh):
    ndev = mesh.shape["lon"]
    lon = P(None, "lon", None)
    return jax.shard_map(functools.partial(local, ndev), mesh=mesh, in_specs=(lon, lon, P(), P(), P()),
                         out_specs=lon, check_vma=False)
```

```python
import functools

import jax
import jax.numpy as jnp
from jax import lax
from jax.experimental import pallas as pl
from jax.experimental.pallas import tpu as pltpu
from jax.sharding import PartitionSpec as P

MESH = pl.DeviceIdType.MESH
F32 = jnp.float32
BF16 = jnp.bfloat16
R = 16
MOST = 8
PIECES = (20, 19, 17, 26)
LANES = 128
W = 15


def reverse_rows(v):
    row = lax.broadcasted_iota(jnp.int32, v.shape, 1)
    v = pltpu.roll(v, 4, 1)
    v = jnp.where((row & 2) == 0, pltpu.roll(v, 6, 1), pltpu.roll(v, 2, 1))
    return jnp.where((row & 1) == 0, pltpu.roll(v, 7, 1), pltpu.roll(v, 1, 1))


def parcels(n, c):
    tail = c - LANES - 64
    share = LANES // tail
    parts, spans, first = [], [], 0
    for columns in (list(range(W)) + list(range(n - W, n)), list(range(W, n - W))):
        half = len(columns) // 2
        pairs = list(zip(columns[:half], columns[half:]))
        rests = [columns[k:k + share] for k in range(0, len(columns), share)]
        count = len(columns) + half + len(rests)
        parts.append((first, columns, pairs, rests))
        spans.append((first, count))
        first += count
    return parts, spans


def gelu(x):
    return 0.5 * x * (1.0 + jnp.tanh(0.7978845608028654 * (x + 0.044715 * (x * x * x))))


def kernel(ndev, n, field, south, sign, weights, bias, out, wf, wh, wl, slab, xh, xl, gain, raw, parcel, landed,
           wsem, lsem, ssem, rsem):
    me = lax.axis_index("lon")
    right, left, twin = lax.rem(me + 1, ndev), lax.rem(me + ndev - 1, ndev), ndev - 1 - me
    total = n + 2 * W

    barrier = pltpu.get_barrier_semaphore()
    for peer in (left, right, twin):
        pl.semaphore_signal(barrier, inc=1, device_id=(peer,), device_id_type=MESH)

    loads = [pltpu.make_async_copy(weights.at[pl.ds(9 * l, 9)], wf.at[pl.ds(9 * l, 9)], wsem.at[l]) for l in range(4)]
    loads[0].start()
    own = [pltpu.make_async_copy(field, slab.at[0, 0, pl.ds(W, n), pl.ds(8, R)], lsem.at[0]),
           pltpu.make_async_copy(south, slab.at[0, 0, pl.ds(W, n), pl.ds(0, 8)], lsem.at[1])]
    for c in own:
        c.start()
    for c in loads[1:]:
        c.start()

    def remote(src, dst, k, peer):
        return pltpu.make_async_remote_copy(src_ref=src, dst_ref=dst, send_sem=ssem.at[k], recv_sem=rsem.at[k],
                                            device_id=(peer,), device_id_type=MESH)

    parts, spans = parcels(n, field.shape[-1])
    tail = field.shape[-1] - LANES - 64

    def pack(half):
        rows = pl.ds(16 - 8 * half, 8)
        lane = lax.broadcasted_iota(jnp.int32, (8, LANES), 1)
        blank = jnp.zeros((8, LANES - 64 - tail), F32)

        def upper_lanes(j):
            return jnp.concatenate([slab[0, 0, W + j, rows, LANES:], blank], axis=1)

        for first, columns, pairs, rests in parts:
            t = first
            for j in columns:
                parcel[half, t] = slab[0, 0, W + j, rows, :LANES]
                t += 1
            for j, k in pairs:
                parcel[half, t] = jnp.where(lane < 64, upper_lanes(j), pltpu.roll(upper_lanes(k), 64, 1))
                t += 1
            for some in rests:
                v = pltpu.roll(upper_lanes(some[0]), 64, 1)
                for k, j in enumerate(some[1:], 1):
                    v = jnp.where(lane < tail * k, v, pltpu.roll(upper_lanes(j), (64 + tail * k) % LANES, 1))
                parcel[half, t] = v
                t += 1

    def unpack(half, part):
        rows = pl.ds(16 - 8 * half, 8)
        lane = lax.broadcasted_iota(jnp.int32, (8, LANES), 1)
        first, columns, pairs, rests = parts[part]
        t = first
        for j in columns:
            slab[1, 0, W + j, rows, :LANES] = landed[half, t]
            t += 1
        wide = {}
        for pair in pairs:
            v = landed[half, t]
            wide[pair[0]], wide[pair[1]] = v, pltpu.roll(v, 64, 1)
            t += 1
        for some in rests:
            v = landed[half, t]
            for k, j in enumerate(some):
                last = pltpu.roll(v, (64 - tail * k) % LANES, 1)
                slab[1, 0, W + j, rows, LANES:] = jnp.where(lane < 64, wide[j], last)[:, :64 + tail]
            t += 1

    def parcel_copy(half, part, k):
        first, count = spans[part]
        place = (half, pl.ds(first, count), pl.ds(half, 8 - half))
        return remote(parcel.at[place], landed.at[place], k, twin)

    fold = [[parcel_copy(half, part, (0, 1, 10, 11)[2 * half + part]) for part in range(2)] for half in range(2)]
    edge = [remote(field.at[pl.ds(n - W, W)], slab.at[0, 0, pl.ds(0, W), pl.ds(8, R)], 2, right),
            remote(field.at[pl.ds(0, W)], slab.at[0, 0, pl.ds(W + n, W), pl.ds(8, R)], 3, left),
            remote(south.at[pl.ds(n - W, W)], slab.at[0, 0, pl.ds(0, W), pl.ds(0, 8)], 4, right),
            remote(south.at[pl.ds(0, W)], slab.at[0, 0, pl.ds(W + n, W), pl.ds(0, 8)], 5, left)]

    def onward(row, k):
        rows = pl.ds(row, 8)
        return [remote(slab.at[1, 0, pl.ds(n, W), rows], slab.at[1, 0, pl.ds(0, W), rows], k, left),
                remote(slab.at[1, 0, pl.ds(W, W), rows], slab.at[1, 0, pl.ds(W + n, W), rows], k + 1, right)]

    upper, lower = onward(16, 6), onward(8, 8)

    own[0].wait()
    pack(0)
    pack(1)
    pl.semaphore_wait(barrier, 3)
    for c in edge:
        c.start()
    for c in fold[0]:
        c.start()

    def prepare(l):
        loads[l].wait()

        def one(t, _):
            w = wf[t]
            hi = w.astype(BF16)
            wh[t] = hi
            wl[t] = (w - hi.astype(F32)).astype(BF16)
            return 0

        lax.fori_loop(9 * l, 9 * l + 9, one, 0)

    def group(count):
        return max(g for g in range(1, MOST + 1) if count % g == 0)

    def north(side, l):
        first = 2 ** l - 1
        count = total - 2 * first
        g = group(count)

        def one(j, _):
            start = first + g * j
            v = slab[1 - side, l, pl.ds(total - g - start, g), pl.ds(16, 8), :]
            v = reverse_rows(v) * sign[...]
            for k in range(g):
                slab[side, l, pl.ds(start + k, 1), pl.ds(24, 8), :] = v[g - 1 - k:g - k]
            return 0

        lax.fori_loop(0, count // g, one, 0)

    def build(l, windows, cols, at):
        s = 2 ** l
        count = cols + 2 * s
        g = group(count)

        def one(j, _):
            for a in range(3):
                x = jnp.concatenate([slab[side, l, pl.ds(col - s + g * j, g), pl.ds(row + (a - 1) * s, 8), :]
                                     for side, row, col in windows], axis=1)
                hi = x.astype(BF16)
                xh[a, pl.ds(at + g * j, g)] = hi
                xl[a, pl.ds(at + g * j, g)] = (x - hi.astype(F32)).astype(BF16)
            return 0

        lax.fori_loop(0, count // g, one, 0)

    def update(l, windows, cols, at):
        g = group(cols)

        def one(j, _):
            for k, (side, row, col) in enumerate(windows):
                place = pl.ds(col + g * j, g)
                new = slab[side, l, place, pl.ds(row, 8), :] + gain[pl.ds(at + g * j, g), pl.ds(8 * k, 8), :]
                if l == 3:
                    out[pl.ds(col - W + g * j, g), pl.ds(row - 8, 8), :] = new
                else:
                    slab[side, l + 1, place, pl.ds(row, 8), :] = new
            return 0

        lax.fori_loop(0, cols // g, one, 0)

    def products(l, start, slot):
        s, piece = 2 ** l, PIECES[l]
        d = None
        for i in range(9):
            a, b = i // 3, i % 3
            rows = pl.ds(start + b * s, piece)
            h = xh[a, rows].reshape(piece * R, -1)
            lo = xl[a, rows].reshape(piece * R, -1)
            for x, w in ((h, wh), (lo, wh), (h, wl)):
                e = jnp.dot(x, w[9 * l + i], preferred_element_type=F32)
                d = e if d is None else d + e
        raw[slot, pl.ds(0, piece * R)] = d

    def finish(l, start, slot):
        piece = PIECES[l]
        g = gelu(raw[slot, pl.ds(0, piece * R)] + bias[pl.ds(l, 1)])
        gain[pl.ds(start, piece)] = g.reshape(piece, R, -1)

    def convolve(l, cols):
        piece = PIECES[l]
        pieces = (cols + piece - 1) // piece

        def place(q):
            return jnp.maximum(jnp.minimum(q * piece, cols - piece), 0)

        def one(q, _):
            finish(l, place(q - 1), (q + 1) % 2)
            products(l, place(q), q % 2)
            return 0

        lax.fori_loop(0, pieces, one, 0)
        finish(l, place(pieces - 1), (pieces + 1) % 2)

    c1, c2, c3 = 1, 3, 7
    n1, n2, n3 = total - 2, total - 6, total - 14
    S8, S16, M16 = (0, 8), (0, 16), (1, 16)

    def pair(x, y, c):
        return [x + (c,), y + (c,)]

    def halves(x, c, m):
        return [x + (c,), x + (c + m // 2,)]

    def start_all(copies):
        for c in copies:
            c.start()

    def wait_all(copies):
        for c in copies:
            c.wait()

    def south_rows(cols):
        for l in range(1, 4):
            slab[0, l, cols, pl.ds(0, 8), :] = slab[0, 0, cols, pl.ds(0, 8), :]

    def first():
        own[1].wait()
        south_rows(pl.ds(W, n))
        for l in range(1, 4):
            slab[1, l, :, pl.ds(0, 8), :] = zero

    def halo_here():
        wait_all(edge)
        south_rows(pl.ds(0, W))
        south_rows(pl.ds(W + n, W))

    def upper_sent():
        fold[0][0].wait()
        unpack(0, 0)
        start_all(upper)
        fold[1][0].start()

    def upper_here():
        fold[0][1].wait()
        unpack(0, 1)
        wait_all(upper)
        fold[1][1].start()
        north(0, 0)
        north(1, 0)

    def lower_sent():
        fold[1][0].wait()
        unpack(1, 0)
        start_all(lower)
        north(0, 2)

    def lower_here():
        fold[1][1].wait()
        unpack(1, 1)
        wait_all(lower)
        north(1, 2)

    def split(layer, c, m):
        middle = n - 2 * c
        return ([(pair(S8, S16, W + c), middle)],
                [(pair(S8, S16, c), W), (pair(S8, S16, W + c + middle), W)])

    middle0, sides0 = split(0, c1, n1)
    middle1, sides1 = split(1, c2, n2)
    steps = [
        (0, middle0, first),
        (1, middle1, None),
        (0, sides0, halo_here),
        (1, sides1, None),
        (2, [(halves(S8, c3, n3), n3 // 2)], upper_sent),
        (0, [(pair(S16, (1, 17), c1), n1)], upper_here),
        (1, [(pair(S16, M16, c2), n2)], lambda: (north(0, 1), north(1, 1))),
        (2, [(halves(S16, c3, n3), n3 // 2)], lower_sent),
        (0, [(halves((1, 9), c1, n1), n1 // 2)], lower_here),
        (1, [(halves((1, 12), c2, n2), n2 // 2)], None),
        (2, [(halves(M16, c3, n3), n3 // 2)], None),
        (3, [(pair(S8, S16, W), n)], lambda: north(0, 3)),
    ]

    def placed(layer, segments):
        at, result = 0, []
        for windows, count in segments:
            result.append((windows, count, at))
            at += count + 2 ** (layer + 1)
        return result, at - 2 ** (layer + 1)

    zero = jnp.zeros((total, 8, slab.shape[-1]), F32)
    slab[1, 0, :, pl.ds(0, 8), :] = zero
    for l in range(4):
        prepare(l)

    def step(p, _):
        l = jnp.int32(0)
        cols = jnp.int32(0)
        for k, (layer, segments, before) in enumerate(steps):
            @pl.when(p == k)
            def _():
                if before is not None:
                    before()
                for segment in placed(layer, segments)[0]:
                    build(layer, *segment)

            l = jnp.where(p == k, layer, l)
            cols = jnp.where(p == k, placed(layer, segments)[1], cols)
        for layer in range(4):
            @pl.when(l == layer)
            def _():
                convolve(layer, cols)
        for k, (layer, segments, before) in enumerate(steps):
            @pl.when(p == k)
            def _():
                for segment in placed(layer, segments)[0]:
                    update(layer, *segment)
        return 0

    lax.fori_loop(0, len(steps), step, 0)


def local(ndev, field, south, sign, weights, bias):
    rows, n, c = field.shape
    total = n + 2 * W
    weights = weights.reshape(-1, c, c)
    tiles = sum(count for _, count in parcels(n, c)[1])
    taps = weights.shape[0]
    any_ = pl.BlockSpec(memory_space=pl.ANY)
    vmem = pl.BlockSpec(memory_space=pltpu.VMEM)
    result = pl.pallas_call(
        functools.partial(kernel, ndev, n),
        out_shape=jax.ShapeDtypeStruct((n, rows, c), F32),
        in_specs=[any_, any_, vmem, any_, vmem],
        out_specs=vmem,
        scratch_shapes=[
            pltpu.VMEM((taps, c, c), F32),
            pltpu.VMEM((taps, c, c), BF16),
            pltpu.VMEM((taps, c, c), BF16),
            pltpu.VMEM((2, 4, total, 32, c), F32),
            pltpu.VMEM((3, total, R, c), BF16),
            pltpu.VMEM((3, total, R, c), BF16),
            pltpu.VMEM((total, R, c), F32),
            pltpu.VMEM((2, max(PIECES) * R, c), F32),
            pltpu.VMEM((2, tiles, 8, LANES), F32),
            pltpu.VMEM((2, tiles, 8, LANES), F32),
            pltpu.SemaphoreType.DMA((4,)),
            pltpu.SemaphoreType.DMA((2,)),
            pltpu.SemaphoreType.DMA((12,)),
            pltpu.SemaphoreType.DMA((12,)),
        ],
        compiler_params=pltpu.CompilerParams(collective_id=0, has_side_effects=True, vmem_limit_bytes=60 << 20),
    )(field.transpose(1, 0, 2), south.transpose(1, 0, 2), sign.astype(F32).reshape(1, -1), weights, bias)
    return result.transpose(1, 0, 2)


def solution(mesh):
    ndev = mesh.shape["lon"]
    lon = P(None, "lon", None)
    return jax.shard_map(functools.partial(local, ndev), mesh=mesh, in_specs=(lon, lon, P(), P(), P()),
                         out_specs=lon, check_vma=False)
```

```python
import functools

import jax
import jax.numpy as jnp
from jax import lax
from jax.experimental import pallas as pl
from jax.experimental.pallas import tpu as pltpu
from jax.sharding import PartitionSpec as P

MESH = pl.DeviceIdType.MESH
F32 = jnp.float32
BF16 = jnp.bfloat16
R = 16
MOST = 8
PIECES = (20, 19, 34, 26)
LANES = 128
W = 15


def reverse_rows(v):
    row = lax.broadcasted_iota(jnp.int32, v.shape, 1)
    v = pltpu.roll(v, 4, 1)
    v = jnp.where((row & 2) == 0, pltpu.roll(v, 6, 1), pltpu.roll(v, 2, 1))
    return jnp.where((row & 1) == 0, pltpu.roll(v, 7, 1), pltpu.roll(v, 1, 1))


def parcels(n, c):
    tail = c - LANES - 64
    share = LANES // tail
    parts, spans, first = [], [], 0
    for columns in (list(range(W)) + list(range(n - W, n)), list(range(W, n - W))):
        half = len(columns) // 2
        pairs = list(zip(columns[:half], columns[half:]))
        rests = [columns[k:k + share] for k in range(0, len(columns), share)]
        count = len(columns) + half + len(rests)
        parts.append((first, columns, pairs, rests))
        spans.append((first, count))
        first += count
    return parts, spans


def gelu(x):
    return 0.5 * x * (1.0 + jnp.tanh(0.7978845608028654 * (x + 0.044715 * (x * x * x))))


def kernel(ndev, n, field, south, sign, weights, bias, out, wf, wh, wl, slab, xh, xl, gain, raw, parcel, landed,
           wsem, lsem, ssem, rsem):
    me = lax.axis_index("lon")
    right, left, twin = lax.rem(me + 1, ndev), lax.rem(me + ndev - 1, ndev), ndev - 1 - me
    total = n + 2 * W

    barrier = pltpu.get_barrier_semaphore()
    for peer in (left, right, twin):
        pl.semaphore_signal(barrier, inc=1, device_id=(peer,), device_id_type=MESH)

    loads = [pltpu.make_async_copy(weights.at[pl.ds(9 * l, 9)], wf.at[pl.ds(9 * l, 9)], wsem.at[l]) for l in range(4)]
    loads[0].start()
    own = [pltpu.make_async_copy(field, slab.at[0, 0, pl.ds(W, n), pl.ds(8, R)], lsem.at[0]),
           pltpu.make_async_copy(south, slab.at[0, 0, pl.ds(W, n), pl.ds(0, 8)], lsem.at[1])]
    for c in own:
        c.start()
    for c in loads[1:]:
        c.start()

    def remote(src, dst, k, peer):
        return pltpu.make_async_remote_copy(src_ref=src, dst_ref=dst, send_sem=ssem.at[k], recv_sem=rsem.at[k],
                                            device_id=(peer,), device_id_type=MESH)

    parts, spans = parcels(n, field.shape[-1])
    tail = field.shape[-1] - LANES - 64

    def pack(half):
        rows = pl.ds(16 - 8 * half, 8)
        lane = lax.broadcasted_iota(jnp.int32, (8, LANES), 1)
        blank = jnp.zeros((8, LANES - 64 - tail), F32)

        def upper_lanes(j):
            return jnp.concatenate([slab[0, 0, W + j, rows, LANES:], blank], axis=1)

        for first, columns, pairs, rests in parts:
            t = first
            for j in columns:
                parcel[half, t] = slab[0, 0, W + j, rows, :LANES]
                t += 1
            for j, k in pairs:
                parcel[half, t] = jnp.where(lane < 64, upper_lanes(j), pltpu.roll(upper_lanes(k), 64, 1))
                t += 1
            for some in rests:
                v = pltpu.roll(upper_lanes(some[0]), 64, 1)
                for k, j in enumerate(some[1:], 1):
                    v = jnp.where(lane < tail * k, v, pltpu.roll(upper_lanes(j), (64 + tail * k) % LANES, 1))
                parcel[half, t] = v
                t += 1

    def unpack(half, part):
        rows = pl.ds(16 - 8 * half, 8)
        lane = lax.broadcasted_iota(jnp.int32, (8, LANES), 1)
        first, columns, pairs, rests = parts[part]
        t = first
        for j in columns:
            slab[1, 0, W + j, rows, :LANES] = landed[half, t]
            t += 1
        wide = {}
        for pair in pairs:
            v = landed[half, t]
            wide[pair[0]], wide[pair[1]] = v, pltpu.roll(v, 64, 1)
            t += 1
        for some in rests:
            v = landed[half, t]
            for k, j in enumerate(some):
                last = pltpu.roll(v, (64 - tail * k) % LANES, 1)
                slab[1, 0, W + j, rows, LANES:] = jnp.where(lane < 64, wide[j], last)[:, :64 + tail]
            t += 1

    def parcel_copy(half, part, k):
        first, count = spans[part]
        place = (half, pl.ds(first, count), pl.ds(half, 8 - half))
        return remote(parcel.at[place], landed.at[place], k, twin)

    fold = [[parcel_copy(half, part, (0, 1, 10, 11)[2 * half + part]) for part in range(2)] for half in range(2)]
    edge = [remote(field.at[pl.ds(n - W, W)], slab.at[0, 0, pl.ds(0, W), pl.ds(8, R)], 2, right),
            remote(field.at[pl.ds(0, W)], slab.at[0, 0, pl.ds(W + n, W), pl.ds(8, R)], 3, left),
            remote(south.at[pl.ds(n - W, W)], slab.at[0, 0, pl.ds(0, W), pl.ds(0, 8)], 4, right),
            remote(south.at[pl.ds(0, W)], slab.at[0, 0, pl.ds(W + n, W), pl.ds(0, 8)], 5, left)]

    def onward(row, count, k):
        rows = pl.ds(row, count)
        return [remote(slab.at[1, 0, pl.ds(n, W), rows], slab.at[1, 0, pl.ds(0, W), rows], k, left),
                remote(slab.at[1, 0, pl.ds(W, W), rows], slab.at[1, 0, pl.ds(W + n, W), rows], k + 1, right)]

    upper, lower = onward(16, 8, 6), onward(9, 7, 8)

    own[0].wait()
    pack(0)
    pack(1)
    pl.semaphore_wait(barrier, 3)
    for c in edge:
        c.start()
    for c in fold[0]:
        c.start()

    def prepare(l):
        loads[l].wait()

        def one(t, _):
            w = wf[t]
            hi = w.astype(BF16)
            wh[t] = hi
            wl[t] = (w - hi.astype(F32)).astype(BF16)
            return 0

        lax.fori_loop(9 * l, 9 * l + 9, one, 0)

    def group(count):
        return max(g for g in range(1, MOST + 1) if count % g == 0)

    def north(side, l):
        first = 2 ** l - 1
        count = total - 2 * first
        g = group(count)

        def one(j, _):
            start = first + g * j
            v = slab[1 - side, l, pl.ds(total - g - start, g), pl.ds(16, 8), :]
            v = reverse_rows(v) * sign[...]
            for k in range(g):
                slab[side, l, pl.ds(start + k, 1), pl.ds(24, 8), :] = v[g - 1 - k:g - k]
            return 0

        lax.fori_loop(0, count // g, one, 0)

    def build(l, windows, cols, at):
        s = 2 ** l
        count = cols + 2 * s
        g = group(count)

        def one(j, _):
            for a in range(3):
                x = jnp.concatenate([slab[side, l, pl.ds(col - s + g * j, g), pl.ds(row + (a - 1) * s, 8), :]
                                     for side, row, col in windows], axis=1)
                hi = x.astype(BF16)
                xh[a, pl.ds(at + g * j, g)] = hi
                xl[a, pl.ds(at + g * j, g)] = (x - hi.astype(F32)).astype(BF16)
            return 0

        lax.fori_loop(0, count // g, one, 0)

    def update(l, windows, cols, at):
        g = group(cols)

        def one(j, _):
            for k, (side, row, col) in enumerate(windows):
                place = pl.ds(col + g * j, g)
                new = slab[side, l, place, pl.ds(row, 8), :] + gain[pl.ds(at + g * j, g), pl.ds(8 * k, 8), :]
                if l == 3:
                    out[pl.ds(col - W + g * j, g), pl.ds(row - 8, 8), :] = new
                else:
                    slab[side, l + 1, place, pl.ds(row, 8), :] = new
            return 0

        lax.fori_loop(0, cols // g, one, 0)

    def products(l, start, slot):
        s, piece = 2 ** l, PIECES[l]
        d = None
        for i in range(9):
            a, b = i // 3, i % 3
            rows = pl.ds(start + b * s, piece)
            h = xh[a, rows].reshape(piece * R, -1)
            lo = xl[a, rows].reshape(piece * R, -1)
            for x, w in ((h, wh), (lo, wh), (h, wl)):
                e = jnp.dot(x, w[9 * l + i], preferred_element_type=F32)
                d = e if d is None else d + e
        raw[slot, pl.ds(0, piece * R)] = d

    def finish(l, start, slot):
        piece = PIECES[l]
        g = gelu(raw[slot, pl.ds(0, piece * R)] + bias[pl.ds(l, 1)])
        gain[pl.ds(start, piece)] = g.reshape(piece, R, -1)

    def convolve(l, cols):
        piece = PIECES[l]
        pieces = (cols + piece - 1) // piece

        def place(q):
            return jnp.maximum(jnp.minimum(q * piece, cols - piece), 0)

        def one(q, _):
            finish(l, place(q - 1), (q + 1) % 2)
            products(l, place(q), q % 2)
            return 0

        lax.fori_loop(0, pieces, one, 0)
        finish(l, place(pieces - 1), (pieces + 1) % 2)

    c1, c2, c3 = 1, 3, 7
    n1, n2, n3 = total - 2, total - 6, total - 14
    S8, S16, M16 = (0, 8), (0, 16), (1, 16)

    def pair(x, y, c):
        return [x + (c,), y + (c,)]

    def halves(x, c, m):
        return [x + (c,), x + (c + m // 2,)]

    def start_all(copies):
        for c in copies:
            c.start()

    def wait_all(copies):
        for c in copies:
            c.wait()

    def south_rows(cols):
        for l in range(1, 4):
            slab[0, l, cols, pl.ds(0, 8), :] = slab[0, 0, cols, pl.ds(0, 8), :]

    def first():
        own[1].wait()
        south_rows(pl.ds(W, n))
        for l in range(1, 4):
            slab[1, l, :, pl.ds(0, 8), :] = zero

    def halo_here():
        wait_all(edge)
        south_rows(pl.ds(0, W))
        south_rows(pl.ds(W + n, W))

    def upper_sent():
        fold[0][0].wait()
        unpack(0, 0)
        start_all(upper)
        fold[1][0].start()

    def upper_here():
        fold[0][1].wait()
        unpack(0, 1)
        wait_all(upper)
        fold[1][1].start()
        north(0, 0)
        north(1, 0)

    def lower_sent():
        fold[1][0].wait()
        unpack(1, 0)
        start_all(lower)
        north(0, 2)

    def lower_here():
        fold[1][1].wait()
        unpack(1, 1)
        wait_all(lower)
        north(1, 2)

    def split(layer, c, m):
        middle = n - 2 * c
        return ([(pair(S8, S16, W + c), middle)],
                [(pair(S8, S16, c), W), (pair(S8, S16, W + c + middle), W)])

    middle0, sides0 = split(0, c1, n1)
    middle1, sides1 = split(1, c2, n2)
    steps = [
        (0, middle0, first),
        (1, middle1, None),
        (0, sides0, halo_here),
        (1, sides1, None),
        (2, [(halves(S8, c3, n3), n3 // 2)], upper_sent),
        (0, [(pair(S16, (1, 17), c1), n1)], upper_here),
        (1, [(pair(S16, M16, c2), n2)], lambda: (north(0, 1), north(1, 1))),
        (2, [(halves(S16, c3, n3), n3 // 2)], lower_sent),
        (0, [(halves((1, 9), c1, n1), n1 // 2)], lower_here),
        (1, [(halves((1, 12), c2, n2), n2 // 2)], None),
        (2, [(halves(M16, c3, n3), n3 // 2)], None),
        (3, [(pair(S8, S16, W), n)], lambda: north(0, 3)),
    ]

    def placed(layer, segments):
        at, result = 0, []
        for windows, count in segments:
            result.append((windows, count, at))
            at += count + 2 ** (layer + 1)
        return result, at - 2 ** (layer + 1)

    zero = jnp.zeros((total, 8, slab.shape[-1]), F32)
    slab[1, 0, :, pl.ds(0, 8), :] = zero
    for l in range(4):
        prepare(l)

    def step(p, _):
        l = jnp.int32(0)
        cols = jnp.int32(0)
        for k, (layer, segments, before) in enumerate(steps):
            @pl.when(p == k)
            def _():
                if before is not None:
                    before()
                for segment in placed(layer, segments)[0]:
                    build(layer, *segment)

            l = jnp.where(p == k, layer, l)
            cols = jnp.where(p == k, placed(layer, segments)[1], cols)
        for layer in range(4):
            @pl.when(l == layer)
            def _():
                convolve(layer, cols)
        for k, (layer, segments, before) in enumerate(steps):
            @pl.when(p == k)
            def _():
                for segment in placed(layer, segments)[0]:
                    update(layer, *segment)
        return 0

    lax.fori_loop(0, len(steps), step, 0)


def local(ndev, field, south, sign, weights, bias):
    rows, n, c = field.shape
    total = n + 2 * W
    weights = weights.reshape(-1, c, c)
    tiles = sum(count for _, count in parcels(n, c)[1])
    taps = weights.shape[0]
    any_ = pl.BlockSpec(memory_space=pl.ANY)
    vmem = pl.BlockSpec(memory_space=pltpu.VMEM)
    result = pl.pallas_call(
        functools.partial(kernel, ndev, n),
        out_shape=jax.ShapeDtypeStruct((n, rows, c), F32),
        in_specs=[any_, any_, vmem, any_, vmem],
        out_specs=vmem,
        scratch_shapes=[
            pltpu.VMEM((taps, c, c), F32),
            pltpu.VMEM((taps, c, c), BF16),
            pltpu.VMEM((taps, c, c), BF16),
            pltpu.VMEM((2, 4, total, 32, c), F32),
            pltpu.VMEM((3, total, R, c), BF16),
            pltpu.VMEM((3, total, R, c), BF16),
            pltpu.VMEM((total, R, c), F32),
            pltpu.VMEM((2, max(PIECES) * R, c), F32),
            pltpu.VMEM((2, tiles, 8, LANES), F32),
            pltpu.VMEM((2, tiles, 8, LANES), F32),
            pltpu.SemaphoreType.DMA((4,)),
            pltpu.SemaphoreType.DMA((2,)),
            pltpu.SemaphoreType.DMA((12,)),
            pltpu.SemaphoreType.DMA((12,)),
        ],
        compiler_params=pltpu.CompilerParams(collective_id=0, has_side_effects=True, vmem_limit_bytes=60 << 20),
    )(field.transpose(1, 0, 2), south.transpose(1, 0, 2), sign.astype(F32).reshape(1, -1), weights, bias)
    return result.transpose(1, 0, 2)


def solution(mesh):
    ndev = mesh.shape["lon"]
    lon = P(None, "lon", None)
    return jax.shard_map(functools.partial(local, ndev), mesh=mesh, in_specs=(lon, lon, P(), P(), P()),
                         out_specs=lon, check_vma=False)
```
